512 devices in a mesh: blk: 16 (over x_lo, y, core), chan: 32 (over z, x_hi).
Axes of the slice: x: 4 (x_hi: 2, x_lo: 2; x = x_hi * 2 + x_lo), y: 4, z: 16, core: 2. Of those that a mesh axis runs over, the one named last changes fastest.
Arguments:
- react_basis: bfloat16 [256, 2048, 128], P('blk', 'chan'), may hold values from -0.03125 to 0.03125
- prod_basis: bfloat16 [512, 2048, 128], P('blk', 'chan'), may hold values from -0.25 to 0.25
- react_radius: float32 [256], replicated, may hold values from 0.5 to 3
- prod_radius: float32 [512], replicated, may hold values from 0.5 to 3
- prod_weight: float32 [512], replicated, may hold values from 0.3 to 3
- angle_cos: float32 [128], replicated, may hold values from -1 to 1
- angle_weight: float32 [128], replicated, may hold values from 0.3 to 3
- coupling: int32 [32, 32], P('blk', 'chan'), may hold values 0 or 1
Outputs:
- kernel: float32 [2048, 2048], P('blk', 'chan')
The draws below stay inside these ranges and needn't reach their ends.
All inputs are finite; a program needn't handle non-finite values. No bound on the sum of `coupling` on one device may be relied on, other than what follows from the above.
Results may differ from the reference program's by a relative error of at most 0.0029.
Values may be sent and summed in bfloat16 or wider, within the bound.
A program may use at most 64 MiB of HBM per device.

```python
import math
import jax
import jax.numpy as jnp
from jax import lax

C = 2048
G = 128
S = 512
NTB = 32
R = 256


def plant(entries, key, least, high):
    spot = [jax.random.randint(jax.random.fold_in(key, axis), (), 0, length) for axis, length in enumerate(entries.shape)]
    main_axis = entries.shape.index(max(entries.shape))
    beside = spot[:main_axis] + [(spot[main_axis] + 1) % entries.shape[main_axis]] + spot[main_axis + 1:]
    return entries.at[tuple(spot)].set(least).at[tuple(beside)].set(high)


def levels(rng, extent, pieces, least, largest):
    loudness = 1.0
    for dim, parts in pieces:
        steps = jax.random.uniform(jax.random.fold_in(jax.random.fold_in(rng, 6), dim), (parts,), jnp.float32, least / len(pieces), largest / len(pieces))
        loudness = loudness * jnp.repeat(jnp.exp(steps), extent[dim] // parts).reshape((-1,) + (1,) * (len(extent) - 1 - dim))
    return loudness


def centred(rng, extent, scale, most, pieces=(), kind=jnp.bfloat16):
    gain = levels(rng, extent, pieces, -0.22, 0.18) if pieces else 1.0
    array = jax.random.normal(rng, extent, jnp.float32) * scale * gain
    return jnp.minimum(jnp.maximum(array, -most), most).astype(kind)


def setup_inputs(seed: int = 0) -> dict:
    streams_of = jax.random.split(jax.random.key(seed), 9)
    return {
        "react_basis": centred(streams_of[0], (R, C, G), (R * G) ** -0.5, 0.03125, ((0, 16), (1, 32))),
        "prod_basis": centred(streams_of[1], (S, C, G), S ** -0.5, 0.25, ((0, 16), (1, 32))),
        "react_radius": jnp.clip(jax.random.uniform(streams_of[2], (R,), jnp.float32, 0.5, 3.0), 0.5, 3.0),
        "prod_radius": jnp.clip(jax.random.uniform(streams_of[3], (S,), jnp.float32, 0.5, 3.0), 0.5, 3.0),
        "prod_weight": jnp.clip(jnp.exp(jax.random.uniform(streams_of[4], (S,), jnp.float32, math.log(0.3), math.log(3.0))), 0.3, 3.0),
        "angle_cos": jnp.clip(jax.random.uniform(streams_of[5], (G,), jnp.float32, -1.0, 1.0), -1.0, 1.0),
        "angle_weight": jnp.clip(jnp.exp(jax.random.uniform(streams_of[6], (G,), jnp.float32, math.log(0.3), math.log(3.0))), 0.3, 3.0),
        "coupling": plant((jax.random.randint(streams_of[7], (NTB, NTB), 0, 4) < 3).astype(jnp.int32), jax.random.fold_in(streams_of[7], 1), 0, 1),
    }


wave_number = 480.0

def reference(react_basis, prod_basis, react_radius, prod_radius, prod_weight, angle_cos, angle_weight, coupling):
    near = react_radius[:, None, None]
    far = prod_radius[None, :, None]
    dist = near * near + far * far - 2.0 * angle_cos[None, None, :] * near * far
    shifted = 1.0 + dist
    weight = angle_weight[None, None, :] * prod_weight[None, :, None] * jnp.cos(wave_number * jnp.sqrt(shifted)) / shifted
    inner = jnp.einsum('rsg,scg->rcg', weight.astype(jnp.float32), prod_basis.astype(jnp.float32), precision=lax.Precision.HIGHEST)
    inner_b = lax.optimization_barrier(inner.astype(jnp.bfloat16))
    flat_inner = jnp.transpose(inner_b, (0, 2, 1)).reshape(R * G, C)
    flat_react = jnp.transpose(react_basis, (0, 2, 1)).reshape(R * G, C)
    full = jnp.dot(flat_inner.T, flat_react, preferred_element_type=jnp.float32)
    tile = C // NTB
    mask = jnp.repeat(jnp.repeat(coupling.astype(jnp.float32), tile, axis=0), tile, axis=1)
    return full * mask
```

```python
import jax
import jax.numpy as jnp
from jax import lax
from jax.experimental import pallas as pl
from jax.experimental.pallas import tpu as pltpu
from jax.sharding import PartitionSpec as P

MESH = pl.DeviceIdType.MESH
F32 = jnp.float32
BF16 = jnp.bfloat16

turns_per_unit = 76.39437268410976
cos_terms = (
    0.9999999890590228,
    -19.739204499454026,
    64.93911745990036,
    -85.45013953095037,
    60.16763095136588,
    -25.96759924965491,
    6.528658162567069,
)
y_order = (2, 1, 3, 0)


def lanes(a, b):
    return jnp.concatenate([a, b], axis=1)


def kernel(
    pr_ref,
    pw_ref,
    rr_ref,
    cos_ref,
    aw_ref,
    r_ref,
    p_ref,
    o_ref,
    s_r,
    s_p,
    pr_t,
    pw_t,
    r_send,
    p_send,
    r_got,
    p_got,
    weight,
    in_send,
    in_got,
    r_row,
    in_row,
    rhs,
    y_send,
    y_got,
    own,
    z_send,
    z_got,
    rb_ss,
    rb_rs,
    pb_ss,
    pb_rs,
    rz_ss,
    rz_rs,
    iz_ss,
    iz_rs,
    rr_ss,
    rr_rs,
    ir_ss,
    ir_rs,
    y_ss,
    y_rs,
    z_ss,
    z_rs,
):
    b = lax.axis_index("blk")
    h = lax.axis_index("chan")
    z, xh = h // 2, h % 2
    xl, y, co = b // 8, (b // 2) % 4, b % 2
    quad = xl * 2 + co

    def at_blk(off):
        return ((b + off) % 16, h)

    def at_z(off):
        return (b, ((z + off) % 16) * 2 + xh)

    def remote(src, dst, ss, rs, dev):
        return pltpu.make_async_remote_copy(
            src_ref=src, dst_ref=dst, send_sem=ss, recv_sem=rs, device_id=dev, device_id_type=MESH
        )

    def row_peer(off):
        j = (xh * 4 + quad + off) % 8
        return j, (((j // 2) % 2) * 8 + y * 2 + j % 2, z * 2 + j // 4)

    barrier = pltpu.get_barrier_semaphore()

    @pl.loop(1, 16)
    def _(off):
        pl.semaphore_signal(barrier, inc=1, device_id=at_blk(off), device_id_type=MESH)
        pl.semaphore_signal(barrier, inc=1, device_id=at_z(off), device_id_type=MESH)

    @pl.loop(0, 4)
    def _(i):
        dev = ((i // 2) * 8 + y * 2 + i % 2, z * 2 + 1 - xh)
        pl.semaphore_signal(barrier, inc=1, device_id=dev, device_id_type=MESH)

    @pl.loop(0, 8)
    def _(i):
        t = r_ref[pl.ds(2 * i, 2)].reshape(128, 128).astype(F32).T
        lo, hi = t[:64], t[64:]
        s_r[pl.ds(2 * i, 64, stride=16), :] = lanes(lo[:, :64], hi[:, :64])
        s_r[pl.ds(2 * i + 1, 64, stride=16), :] = lanes(lo[:, 64:], hi[:, 64:])

    @pl.loop(0, 16)
    def _(d):
        r_send[d] = s_r[pl.ds(pl.multiple_of(64 * d, 64), 64), :].astype(BF16)

    pl.semaphore_wait(barrier, 34)

    @pl.loop(1, 16)
    def _(off):
        d = (b + off) % 16
        remote(r_send.at[d], r_got.at[b], rb_ss.at[off], rb_rs.at[b], at_blk(off)).start()

    r_got[b] = r_send[b]

    @pl.loop(0, 16)
    def _(i):
        x = jnp.concatenate([p_ref[i], p_ref[16 + i]], axis=0)
        s_p[pl.ds(i, 128, stride=16), :] = x.astype(F32).T

    @pl.loop(0, 16)
    def _(off):
        d = (b + off) % 16
        for gh in range(2):
            start = pl.multiple_of(gh * 1024 + 64 * d, 64)
            p_send[d, gh] = s_p[pl.ds(start, 64), :].astype(BF16)

        @pl.when(off > 0)
        def _():
            remote(p_send.at[d], p_got.at[b], pb_ss.at[off], pb_rs.at[b], at_blk(off)).start()

    p_got[b] = p_send[b]

    for k in range(4):
        cols = slice(128 * k, 128 * k + 128)
        pr_t[cols, :] = jnp.broadcast_to(pr_ref[:, cols], (128, 128)).T
        pw_t[cols, :] = jnp.broadcast_to(pw_ref[:, cols], (128, 128)).T

    def make_weight(gi):
        g = (gi % 2) * 64 + 4 * b + gi // 2
        two_cos = 2.0 * cos_ref[g]
        ang = aw_ref[g]

        @pl.loop(0, 16)
        def _(src):
            for sh in range(2):
                rows = pl.ds(pl.multiple_of(src * 32 + sh * 16, 16), 16)
                far = pr_t[rows, :]
                scale = pw_t[rows, :] * ang
                far2 = far * far
                for half in range(2):
                    cols = slice(128 * half, 128 * half + 128)
                    near = rr_ref[:, cols]
                    q = (1.0 + near * near) + far2 - (two_cos * near) * far
                    rs = lax.rsqrt(q)
                    root = q * rs
                    root = root + (0.5 * rs) * (q - root * root)
                    turns = root * turns_per_unit
                    f = turns - jnp.round(turns)
                    u = f * f
                    c = jnp.full_like(u, cos_terms[6])
                    for term in cos_terms[5::-1]:
                        c = c * u + term
                    w = scale * c * (rs * rs)
                    w_hi = w.astype(BF16)
                    w_lo = (w - w_hi.astype(F32)).astype(BF16)
                    at = pl.multiple_of(sh * 256 + src * 16, 16)
                    weight[gi, pl.ds(at, 16), cols] = w_hi
                    weight[gi, pl.ds(at + 512, 16), cols] = w_lo

    @pl.loop(0, 4)
    def _(gi):
        make_weight(gi)

    @pl.loop(0, 4)
    def _(t):
        qd = (b // 4 + t) % 4

        @pl.loop(0, 4)
        def _(i):
            src = qd * 4 + i

            @pl.when(src != b)
            def _():
                remote(r_send.at[0], r_got.at[src], rb_ss.at[0], rb_rs.at[src], at_blk(1)).wait_recv()

        @pl.loop(0, 4)
        def _(jj):
            j = (z // 4 + 2 + jj) % 4
            k = j * 4 + qd
            block = r_got.at[pl.ds(qd * 4, 4), pl.ds(pl.multiple_of(16 * j, 16), 16), :]

            @pl.when(k != z)
            def _():
                remote(block, r_row.at[quad, z], rz_ss.at[k], rz_rs.at[z], (b, k * 2 + xh)).start()

            @pl.when(k == z)
            def _():
                r_row[quad, z] = block[...]

    @pl.loop(4, 8)
    def _(gi):
        make_weight(gi)

    @pl.loop(1, 16)
    def _(off):
        src = (b + off) % 16
        remote(p_send.at[0], p_got.at[src], pb_ss.at[0], pb_rs.at[src], at_blk(1)).wait_recv()

    @pl.loop(0, 4)
    def _(t):
        j = (z // 4 + 2 + t) % 4
        parts = []
        for gh in range(2):
            x = p_got[:, gh, pl.ds(pl.multiple_of(16 * j, 16), 16), :].reshape(256, 128)
            xt = x.T
            lhs = jnp.concatenate([xt[:64], xt[64:], xt[:64], xt[64:]], axis=1)
            parts.append(jnp.dot(lhs, weight[j * 2 + gh], preferred_element_type=F32))
        for qd in range(4):
            cols = slice(64 * qd, 64 * qd + 64)
            in_send[j * 4 + qd] = lanes(parts[0][:, cols], parts[1][:, cols]).astype(BF16)

        @pl.loop(0, 4)
        def _(qd):
            k = j * 4 + qd

            @pl.when(k != z)
            def _():
                remote(in_send.at[k], in_got.at[z], iz_ss.at[k], iz_rs.at[z], (b, k * 2 + xh)).start()

            @pl.when(k == z)
            def _():
                in_got[z] = in_send[z]

    @pl.loop(1, 16)
    def _(off):
        src = (z + off) % 16
        remote(r_row.at[0, 0], r_row.at[quad, src], rz_ss.at[0], rz_rs.at[src], at_z(1)).wait_recv()

    def quad_peer(off):
        q = (quad + off) % 4
        return q, ((q // 2) * 8 + y * 2 + q % 2, h)

    @pl.loop(1, 4)
    def _(off):
        _, dev = quad_peer(off)
        remote(r_row.at[quad], r_row.at[quad], rr_ss.at[off], rr_rs.at[quad], dev).start()

    me = xh * 4 + quad
    for t in range(4):
        yt = (y + y_order[t]) % 4

        @pl.loop(0, 4)
        def _(i):
            src = (i // 2) * 8 + yt * 2 + i % 2

            @pl.when(src != z)
            def _():
                remote(in_send.at[0], in_got.at[src], iz_ss.at[0], iz_rs.at[src], at_z(1)).wait_recv()

        rows = pl.ds(pl.multiple_of(xh * 64, 64), 64)
        cols = pl.ds(pl.multiple_of(quad * 128, 128), 128)

        @pl.loop(1, 8)
        def _(off):
            j, dev = row_peer(off)
            src = ((j // 2) % 2) * 8 + yt * 2 + j % 2
            remote(in_got.at[src], in_row.at[t, rows, cols], ir_ss.at[t, off], ir_rs.at[t, me], dev).start()

        in_row[t, rows, cols] = in_got[xl * 8 + yt * 2 + co]

    @pl.loop(1, 4)
    def _(off):
        q, dev = quad_peer(off)
        remote(r_row.at[0], r_row.at[q], rr_ss.at[0], rr_rs.at[q], dev).wait_recv()

    @pl.loop(0, 4)
    def _(q):
        for n in range(8):
            x0 = r_row[q, 2 * n].reshape(64, 128)
            x1 = r_row[q, 2 * n + 1].reshape(64, 128)
            at = pl.multiple_of(q * 128, 128)
            cols = slice(128 * n, 128 * n + 128)
            rhs[pl.ds(at, 64), cols] = lanes(x0[:, :64], x1[:, :64])
            rhs[pl.ds(at + 64, 64), cols] = lanes(x0[:, 64:], x1[:, 64:])

    for t in range(4):

        @pl.loop(1, 8)
        def _(off):
            j, dev = row_peer(off)
            src_rows = pl.ds(pl.multiple_of((j // 4) * 64, 64), 64)
            src_cols = pl.ds(pl.multiple_of((j % 4) * 128, 128), 128)
            remote(
                in_got.at[0], in_row.at[t, src_rows, src_cols], ir_ss.at[0, 0], ir_rs.at[t, j], dev
            ).wait_recv()

        @pl.loop(0, 4)
        def _(n):
            cols = pl.ds(pl.multiple_of(n * 256, 256), 256)
            part = jnp.dot(in_row[t], rhs[:, cols], preferred_element_type=F32)
            if t < 3:
                y_send[t, :, cols] = part.astype(BF16)
            else:
                own[:, cols] = part

        if t < 3:
            yt = (y + y_order[t]) % 4
            dev = (xl * 8 + yt * 2 + co, h)
            remote(y_send.at[t], y_got.at[t], y_ss.at[t], y_rs.at[t], dev).start()

    for t in range(3):
        dev = (xl * 8 + ((y + y_order[t]) % 4) * 2 + co, h)
        remote(y_send.at[t], y_got.at[t], y_ss.at[t], y_rs.at[t], dev).wait_recv()

    @pl.loop(0, 8)
    def _(i):
        n = (z // 2 + 4 + i) % 8
        cols = pl.ds(pl.multiple_of(n * 128, 128), 128)
        s = own[:, cols]
        for t in range(3):
            s = s + y_got[t, :, cols].astype(F32)
        top, low = s[:64], s[64:]
        z_send[2 * n] = lanes(top[:, :64], low[:, :64]).astype(BF16)
        z_send[2 * n + 1] = lanes(top[:, 64:], low[:, 64:]).astype(BF16)

        @pl.loop(0, 2)
        def _(e):
            k = 2 * n + e

            @pl.when(k != z)
            def _():
                remote(z_send.at[k], z_got.at[z], z_ss.at[k], z_rs.at[z], (b, k * 2 + xh)).start()

            @pl.when(k == z)
            def _():
                z_got[z] = z_send[z]

    @pl.loop(1, 16)
    def _(off):
        src = (z + off) % 16
        remote(z_send.at[0], z_got.at[src], z_ss.at[0], z_rs.at[src], at_z(1)).wait_recv()

    total = z_got[0].astype(F32)
    for k in range(1, 16):
        total = total + z_got[k].astype(F32)
    o_ref[:64, :] = total[:, :64]
    o_ref[64:, :] = total[:, 64:]

    @pl.loop(1, 16)
    def _(off):
        k = (z + off) % 16
        remote(r_send.at[0], r_got.at[0], rb_ss.at[off], rb_rs.at[0], at_blk(1)).wait_send()
        remote(p_send.at[0], p_got.at[0], pb_ss.at[off], pb_rs.at[0], at_blk(1)).wait_send()
        remote(r_got.at[pl.ds(0, 4), pl.ds(0, 16), :], r_row.at[0, 0], rz_ss.at[k], rz_rs.at[0], at_z(1)).wait_send()
        remote(in_send.at[0], in_got.at[0], iz_ss.at[k], iz_rs.at[0], at_z(1)).wait_send()
        remote(z_send.at[0], z_got.at[0], z_ss.at[k], z_rs.at[0], at_z(1)).wait_send()

    @pl.loop(1, 4)
    def _(off):
        remote(r_row.at[0], r_row.at[0], rr_ss.at[off], rr_rs.at[0], at_blk(1)).wait_send()

    for t in range(4):

        @pl.loop(1, 8)
        def _(off):
            remote(in_got.at[0], in_got.at[0], ir_ss.at[t, off], ir_rs.at[t, 0], at_blk(1)).wait_send()

        if t < 3:
            remote(y_send.at[t], y_got.at[t], y_ss.at[t], y_rs.at[t], at_blk(1)).wait_send()


def local(react_basis, prod_basis, react_radius, prod_radius, prod_weight, angle_cos, angle_weight, coupling):
    dma = pltpu.SemaphoreType.DMA
    vmem = pl.BlockSpec(memory_space=pltpu.VMEM)
    smem = pl.BlockSpec(memory_space=pltpu.SMEM)
    full = pl.pallas_call(
        kernel,
        out_shape=jax.ShapeDtypeStruct((128, 64), F32),
        in_specs=[vmem, vmem, vmem, smem, smem, vmem, vmem],
        out_specs=vmem,
        scratch_shapes=[
            pltpu.VMEM((1024, 128), F32),
            pltpu.VMEM((2048, 128), F32),
            pltpu.VMEM((512, 128), F32),
            pltpu.VMEM((512, 128), F32),
            pltpu.VMEM((16, 64, 128), BF16),
            pltpu.VMEM((16, 2, 64, 128), BF16),
            pltpu.VMEM((16, 64, 128), BF16),
            pltpu.VMEM((16, 2, 64, 128), BF16),
            pltpu.VMEM((8, 1024, 256), BF16),
            pltpu.VMEM((16, 64, 128), BF16),
            pltpu.VMEM((16, 64, 128), BF16),
            pltpu.VMEM((4, 16, 4, 16, 128), BF16),
            pltpu.VMEM((4, 128, 512), BF16),
            pltpu.VMEM((512, 1024), BF16),
            pltpu.VMEM((3, 128, 1024), BF16),
            pltpu.VMEM((3, 128, 1024), BF16),
            pltpu.VMEM((128, 1024), F32),
            pltpu.VMEM((16, 64, 128), BF16),
            pltpu.VMEM((16, 64, 128), BF16),
            dma((16,)),
            dma((16,)),
            dma((16,)),
            dma((16,)),
            dma((16,)),
            dma((16,)),
            dma((16,)),
            dma((16,)),
            dma((4,)),
            dma((4,)),
            dma((4, 8)),
            dma((4, 8)),
            dma((3,)),
            dma((3,)),
            dma((16,)),
            dma((16,)),
        ],
        compiler_params=pltpu.CompilerParams(
            collective_id=0, has_side_effects=True, vmem_limit_bytes=48 * 2**20
        ),
        cost_estimate=pl.CostEstimate(flops=10**9, bytes_accessed=10**6, transcendentals=10**6),
    )(
        prod_radius.reshape(1, -1),
        prod_weight.reshape(1, -1),
        react_radius.reshape(1, -1),
        angle_cos,
        angle_weight,
        react_basis,
        prod_basis,
    )
    mask = jnp.repeat(coupling.astype(F32), 64, axis=0)
    return full * mask


def solution(mesh):
    return jax.shard_map(
        local,
        mesh=mesh,
        in_specs=(P("blk", "chan", None), P("blk", "chan", None), P(), P(), P(), P(), P(), P("blk", "chan")),
        out_specs=P("blk", "chan"),
        check_vma=False,
    )
```

```python
import jax
import jax.numpy as jnp
from jax import lax
from jax.experimental import pallas as pl
from jax.experimental.pallas import tpu as pltpu
from jax.sharding import PartitionSpec as P

MESH = pl.DeviceIdType.MESH
F32 = jnp.float32
BF16 = jnp.bfloat16

turns_per_unit = 76.39437268410976
cos_terms = (
    0.9999999890590228,
    -19.739204499454026,
    64.93911745990036,
    -85.45013953095037,
    60.16763095136588,
    -25.96759924965491,
    6.528658162567069,
)
y_order = (2, 1, 3)


def lanes(a, b):
    return jnp.concatenate([a, b], axis=1)


def kernel(
    pr_any,
    pw_any,
    rr_any,
    cos_any,
    aw_any,
    cp_any,
    r_any,
    p_any,
    o_ref,
    pr_ref,
    pw_ref,
    rr_ref,
    cos_ref,
    aw_ref,
    cp_ref,
    r_ref,
    p_ref,
    s_r,
    s_p,
    pr_t,
    pw_t,
    rr_t,
    near_t,
    rz_send,
    rz_got,
    rb_send,
    rb_got,
    r_row,
    rhs,
    p_send,
    p_got,
    weight,
    in_send,
    in_got,
    in_row,
    y_send,
    y_got,
    own,
    z_send,
    z_got,
    in_sem,
    rz_ss,
    rz_rs,
    rb_ss,
    rb_rs,
    rr_ss,
    rr_rs,
    pb_ss,
    pb_rs,
    iz_ss,
    iz_rs,
    ir_ss,
    ir_rs,
    y_ss,
    y_rs,
    z_ss,
    z_rs,
):
    b = lax.axis_index("blk")
    h = lax.axis_index("chan")
    z, xh = h // 2, h % 2
    xl, y, co = b // 8, (b // 2) % 4, b % 2
    quad = xl * 2 + co
    me = xh * 4 + quad

    def at_blk(off):
        return ((b + off) % 16, h)

    def at_z(off):
        return (b, ((z + off) % 16) * 2 + xh)

    def at_y(t):
        return (xl * 8 + ((y + y_order[t]) % 4) * 2 + co, h)

    def remote(src, dst, ss, rs, dev):
        return pltpu.make_async_remote_copy(
            src_ref=src, dst_ref=dst, send_sem=ss, recv_sem=rs, device_id=dev, device_id_type=MESH
        )

    def row_peer(off):
        j = (me + off) % 8
        return j, (((j // 2) % 2) * 8 + y * 2 + j % 2, z * 2 + j // 4)

    def quad_peer(off):
        q = (quad + off) % 4
        return q, ((q // 2) * 8 + y * 2 + q % 2, h)

    loads = [
        pltpu.make_async_copy(src, dst, in_sem.at[n])
        for n, (src, dst) in enumerate(
            [
                (r_any, r_ref),
                (p_any, p_ref),
                (pr_any, pr_ref),
                (pw_any, pw_ref),
                (rr_any, rr_ref),
                (cos_any, cos_ref),
                (aw_any, aw_ref),
                (cp_any, cp_ref),
            ]
        )
    ]
    for load in loads:
        load.start()

    barrier = pltpu.get_barrier_semaphore()

    @pl.loop(1, 16)
    def _(off):
        pl.semaphore_signal(barrier, inc=1, device_id=at_z(off), device_id_type=MESH)
        pl.semaphore_signal(barrier, inc=1, device_id=at_blk(off), device_id_type=MESH)

    @pl.loop(0, 4)
    def _(i):
        dev = ((i // 2) * 8 + y * 2 + i % 2, z * 2 + 1 - xh)
        pl.semaphore_signal(barrier, inc=1, device_id=dev, device_id_type=MESH)

    loads[0].wait()

    @pl.loop(0, 8)
    def _(n):
        t = r_ref[pl.ds(2 * n, 2)].reshape(128, 128).astype(F32).T
        lo, hi = t[:64], t[64:]
        for e, v in enumerate((lanes(lo[:, :64], hi[:, :64]), lanes(lo[:, 64:], hi[:, 64:]))):
            rows = pl.ds(pl.multiple_of((n % 2) * 32 + e * 16, 16), 16)
            for j in range(4):
                rz_send[j * 4 + n // 2, rows, :] = v[16 * j : 16 * j + 16].astype(BF16)

    pl.semaphore_wait(barrier, 34)

    @pl.loop(1, 16)
    def _(off):
        k = (z + off) % 16
        remote(rz_send.at[k], rz_got.at[z], rz_ss.at[off], rz_rs.at[z], at_z(off)).start()

    rz_got[z] = rz_send[z]

    loads[1].wait()

    @pl.loop(0, 16)
    def _(i):
        x = jnp.concatenate([p_ref[i], p_ref[16 + i]], axis=0)
        s_p[pl.ds(i, 128, stride=16), :] = x.astype(F32).T

    @pl.loop(0, 16)
    def _(off):
        d = (b + off) % 16
        for gh in range(2):
            for j in range(4):
                start = pl.multiple_of((gh * 64 + j * 16 + d) * 16, 16)
                p_send[d, gh, 16 * j : 16 * j + 16, :] = s_p[pl.ds(start, 16), :].astype(BF16)

        @pl.when(off > 0)
        def _():
            remote(p_send.at[d], p_got.at[b], pb_ss.at[off], pb_rs.at[b], at_blk(off)).start()

    p_got[b] = p_send[b]

    for load in loads[2:]:
        load.wait()
    for k in range(4):
        cols = slice(128 * k, 128 * k + 128)
        pr_t[cols, :] = jnp.broadcast_to(pr_ref[:, cols], (128, 128)).T
        pw_t[cols, :] = jnp.broadcast_to(pw_ref[:, cols], (128, 128)).T
    for k in range(2):
        cols = slice(128 * k, 128 * k + 128)
        rr_t[cols, :] = jnp.broadcast_to(rr_ref[:, cols], (128, 128)).T
    for qd in range(4):
        for i in range(4):
            near_t[pl.ds(qd * 64 + i, 16, stride=4), :] = rr_t[pl.ds(qd * 4 + i, 16, stride=16), :]
    for k in range(2):
        cols = slice(128 * k, 128 * k + 128)
        rr_t[cols, :] = near_t[cols, :].T

    @pl.loop(0, 8)
    def _(gi):
        g = (gi % 2) * 64 + (gi // 2) * 16 + b
        two_cos = 2.0 * cos_ref[0, g]
        ang = aw_ref[0, g]

        @pl.loop(0, 16)
        def _(src):
            for sh in range(2):
                rows = pl.ds(pl.multiple_of(src * 32 + sh * 16, 16), 16)
                far = pr_t[rows, :]
                scale = pw_t[rows, :] * ang
                far2 = far * far
                for half in range(2):
                    near = rr_t[128 * half : 128 * half + 16, :]
                    q = (1.0 + near * near) + far2 - (two_cos * near) * far
                    rs = lax.rsqrt(q)
                    root = q * rs
                    root = root + (0.5 * rs) * (q - root * root)
                    turns = root * turns_per_unit
                    f = turns - jnp.round(turns)
                    u = f * f
                    c = jnp.full_like(u, cos_terms[6])
                    for term in cos_terms[5::-1]:
                        c = c * u + term
                    w = scale * c * (rs * rs)
                    w_hi = w.astype(BF16)
                    w_lo = (w - w_hi.astype(F32)).astype(BF16)
                    at = pl.multiple_of(sh * 256 + src * 16, 16)
                    cols = slice(128 * half, 128 * half + 128)
                    weight[gi, pl.ds(at, 16), cols] = w_hi
                    weight[gi, pl.ds(at + 512, 16), cols] = w_lo

    @pl.loop(1, 16)
    def _(off):
        src = (b + off) % 16
        remote(p_send.at[0], p_got.at[src], pb_ss.at[0], pb_rs.at[src], at_blk(1)).wait_recv()

    def in_place(k):
        return in_got.at[k // 8, (k // 2) % 4, k % 2]

    def send_integral(k, e):
        rows = slice(32 * e, 32 * e + 32)

        @pl.when(k != z)
        def _():
            remote(
                in_send.at[k, rows], in_place(z).at[rows], iz_ss.at[e, k], iz_rs.at[e, z], (b, k * 2 + xh)
            ).start()

    @pl.loop(0, 4)
    def _(t):
        j = (z // 4 + 2 + t) % 4
        parts = []
        for gh in range(2):
            x = p_got[:, gh, pl.ds(pl.multiple_of(16 * j, 16), 16), :].reshape(256, 128)
            xt = x.T
            lhs = jnp.concatenate([xt[:64], xt[64:], xt[:64], xt[64:]], axis=1)
            parts.append(jnp.dot(lhs, weight[j * 2 + gh], preferred_element_type=F32))
        for qd in range(4):
            cols = slice(64 * qd, 64 * qd + 64)
            in_send[j * 4 + qd] = lanes(parts[0][:, cols], parts[1][:, cols]).astype(BF16)

        @pl.loop(0, 4)
        def _(qd):
            send_integral(j * 4 + qd, 0)

    @pl.loop(0, 16)
    def _(n):
        send_integral(((z // 4 + 2) * 4 + n) % 16, 1)

    in_got[z // 8, (z // 2) % 4, z % 2] = in_send[z]

    @pl.loop(0, 16)
    def _(off):
        src = (z + off) % 16

        @pl.when(off > 0)
        def _():
            remote(rz_send.at[0], rz_got.at[src], rz_ss.at[0], rz_rs.at[src], at_z(1)).wait_recv()

        v = rz_got[src].astype(F32)
        for i in range(4):
            s_r[pl.ds(16 * i + src, 16, stride=64), :] = v[16 * i : 16 * i + 16]

    @pl.loop(0, 16)
    def _(off):
        d = (b + off) % 16
        rb_send[d] = s_r[pl.ds(pl.multiple_of(64 * d, 64), 64), :].astype(BF16)

        @pl.when(off > 0)
        def _():
            remote(rb_send.at[d], rb_got.at[b], rb_ss.at[off], rb_rs.at[b], at_blk(off)).start()

    rb_got[b] = rb_send[b]

    @pl.loop(0, 16)
    def _(off):
        src = (b + off) % 16

        @pl.when(off > 0)
        def _():
            remote(rb_send.at[0], rb_got.at[src], rb_ss.at[0], rb_rs.at[src], at_blk(1)).wait_recv()

        s_r[pl.ds(pl.multiple_of(64 * src, 64), 64), :] = rb_got[src].astype(F32)

    @pl.loop(0, 16)
    def _(k):
        r_row[quad, k] = s_r[pl.ds(k, 64, stride=16), :].astype(BF16)

    @pl.loop(1, 4)
    def _(off):
        _, dev = quad_peer(off)
        remote(r_row.at[quad], r_row.at[quad], rr_ss.at[off], rr_rs.at[quad], dev).start()

    row_cols = pl.ds(pl.multiple_of(quad * 128, 128), 128)

    def integrals_to_row(e):
        rows = slice(32 * e, 32 * e + 32)

        @pl.loop(1, 16)
        def _(off):
            src = (z + off) % 16
            remote(
                in_send.at[0, rows], in_place(src).at[rows], iz_ss.at[e, 0], iz_rs.at[e, src], at_z(1)
            ).wait_recv()

        at = pl.ds(pl.multiple_of(xh * 32, 32), 32)

        @pl.loop(1, 8)
        def _(off):
            j, dev = row_peer(off)
            remote(
                in_got.at[(j // 2) % 2, :, j % 2, rows],
                in_row.at[e, :, at, row_cols],
                ir_ss.at[e, off],
                ir_rs.at[e, me],
                dev,
            ).start()

        in_row[e, :, at, row_cols] = in_got[xl, :, co, rows]

    integrals_to_row(0)

    @pl.loop(1, 4)
    def _(off):
        q, dev = quad_peer(off)
        remote(r_row.at[0], r_row.at[q], rr_ss.at[0], rr_rs.at[q], dev).wait_recv()

    @pl.loop(0, 4)
    def _(q):
        for n in range(8):
            x0 = r_row[q, 2 * n]
            x1 = r_row[q, 2 * n + 1]
            at = pl.multiple_of(q * 128, 128)
            cols = slice(128 * n, 128 * n + 128)
            rhs[pl.ds(at, 64), cols] = lanes(x0[:, :64], x1[:, :64])
            rhs[pl.ds(at + 64, 64), cols] = lanes(x0[:, 64:], x1[:, 64:])

    def share(e):
        @pl.loop(1, 8)
        def _(off):
            j, dev = row_peer(off)
            at = pl.ds(pl.multiple_of((j // 4) * 32, 32), 32)
            cols = pl.ds(pl.multiple_of((j % 4) * 128, 128), 128)
            remote(
                in_got.at[0, :, 0, 0:32], in_row.at[e, :, at, cols], ir_ss.at[e, 0], ir_rs.at[e, j], dev
            ).wait_recv()

        @pl.loop(0, 4)
        def _(n):
            cols = pl.ds(pl.multiple_of(n * 256, 256), 256)
            part = jnp.dot(in_row[e].reshape(256, 512), rhs[:, cols], preferred_element_type=F32)
            own[e, :, cols] = part
            y_send[e, :, :, cols] = part.astype(BF16).reshape(4, 64, 256)

        for t in range(3):
            yt = (y + y_order[t]) % 4
            remote(y_send.at[e, yt], y_got.at[e, t], y_ss.at[e, t], y_rs.at[e, t], at_y(t)).start()

    share(0)

    integrals_to_row(1)
    share(1)

    def plane_sum(e):
        for t in range(3):
            remote(y_send.at[e, 0], y_got.at[e, t], y_ss.at[e, t], y_rs.at[e, t], at_y(t)).wait_recv()

        @pl.loop(0, 8)
        def _(i):
            n = (z // 2 + 4 + i) % 8
            cols = pl.ds(pl.multiple_of(n * 128, 128), 128)
            s = own[e, pl.ds(pl.multiple_of(y * 64, 64), 64), cols]
            for t in range(3):
                s = s + y_got[e, t, :, cols].astype(F32)
            z_send[e, 2 * n] = lanes(s[:32, :64], s[32:, :64]).astype(BF16)
            z_send[e, 2 * n + 1] = lanes(s[:32, 64:], s[32:, 64:]).astype(BF16)

            @pl.loop(0, 2)
            def _(m):
                k = 2 * n + m

                @pl.when(k != z)
                def _():
                    remote(
                        z_send.at[e, k], z_got.at[e, z], z_ss.at[e, k], z_rs.at[e, z], (b, k * 2 + xh)
                    ).start()

                @pl.when(k == z)
                def _():
                    z_got[e, z] = z_send[e, z]

    plane_sum(0)
    plane_sum(1)

    totals = []
    for e in range(2):

        @pl.loop(1, 16)
        def _(off):
            src = (z + off) % 16
            remote(z_send.at[e, 0], z_got.at[e, src], z_ss.at[e, 0], z_rs.at[e, src], at_z(1)).wait_recv()

        total = z_got[e, 0].astype(F32)
        for k in range(1, 16):
            total = total + z_got[e, k].astype(F32)
        totals.append(total)
    out = jnp.concatenate(totals, axis=0).T
    o_ref[...] = lanes(out[:64] * cp_ref[0, 0].astype(F32), out[64:] * cp_ref[0, 1].astype(F32))

    @pl.loop(1, 16)
    def _(off):
        k = (z + off) % 16
        remote(rz_send.at[0], rz_got.at[0], rz_ss.at[off], rz_rs.at[0], at_z(1)).wait_send()
        remote(rb_send.at[0], rb_got.at[0], rb_ss.at[off], rb_rs.at[0], at_blk(1)).wait_send()
        remote(p_send.at[0], p_got.at[0], pb_ss.at[off], pb_rs.at[0], at_blk(1)).wait_send()
        for e in range(2):
            part = in_send.at[0, 0:32]
            remote(part, part, iz_ss.at[e, k], iz_rs.at[e, 0], at_z(1)).wait_send()
            remote(z_send.at[e, 0], z_got.at[e, 0], z_ss.at[e, k], z_rs.at[e, 0], at_z(1)).wait_send()

    @pl.loop(1, 4)
    def _(off):
        remote(r_row.at[0], r_row.at[0], rr_ss.at[off], rr_rs.at[0], at_blk(1)).wait_send()

    for e in range(2):

        @pl.loop(1, 8)
        def _(off):
            part = in_got.at[0, :, 0, 0:32]
            remote(part, part, ir_ss.at[e, off], ir_rs.at[e, 0], at_blk(1)).wait_send()

        for t in range(3):
            remote(y_send.at[e, 0], y_got.at[e, t], y_ss.at[e, t], y_rs.at[e, t], at_blk(1)).wait_send()


def local(react_basis, prod_basis, react_radius, prod_radius, prod_weight, angle_cos, angle_weight, coupling):
    dma = pltpu.SemaphoreType.DMA
    anywhere = pl.BlockSpec(memory_space=pl.ANY)
    full = pl.pallas_call(
        kernel,
        out_shape=jax.ShapeDtypeStruct((64, 128), F32),
        in_specs=[anywhere] * 8,
        out_specs=pl.BlockSpec(memory_space=pltpu.VMEM),
        scratch_shapes=[
            pltpu.VMEM((1, 512), F32),
            pltpu.VMEM((1, 512), F32),
            pltpu.VMEM((1, 256), F32),
            pltpu.SMEM((1, 128), F32),
            pltpu.SMEM((1, 128), F32),
            pltpu.SMEM((1, 2), jnp.int32),
            pltpu.VMEM((16, 64, 128), BF16),
            pltpu.VMEM((32, 64, 128), BF16),
            pltpu.VMEM((1024, 128), F32),
            pltpu.VMEM((2048, 128), F32),
            pltpu.VMEM((512, 128), F32),
            pltpu.VMEM((512, 128), F32),
            pltpu.VMEM((256, 128), F32),
            pltpu.VMEM((256, 128), F32),
            pltpu.VMEM((16, 64, 128), BF16),
            pltpu.VMEM((16, 64, 128), BF16),
            pltpu.VMEM((16, 64, 128), BF16),
            pltpu.VMEM((16, 64, 128), BF16),
            pltpu.VMEM((4, 16, 64, 128), BF16),
            pltpu.VMEM((512, 1024), BF16),
            pltpu.VMEM((16, 2, 64, 128), BF16),
            pltpu.VMEM((16, 2, 64, 128), BF16),
            pltpu.VMEM((8, 1024, 256), BF16),
            pltpu.VMEM((16, 64, 128), BF16),
            pltpu.VMEM((2, 4, 2, 64, 128), BF16),
            pltpu.VMEM((2, 4, 64, 512), BF16),
            pltpu.VMEM((2, 4, 64, 1024), BF16),
            pltpu.VMEM((2, 3, 64, 1024), BF16),
            pltpu.VMEM((2, 256, 1024), F32),
            pltpu.VMEM((2, 16, 32, 128), BF16),
            pltpu.VMEM((2, 16, 32, 128), BF16),
            dma((8,)),
            dma((16,)),
            dma((16,)),
            dma((16,)),
            dma((16,)),
            dma((4,)),
            dma((4,)),
            dma((16,)),
            dma((16,)),
            dma((2, 16)),
            dma((2, 16)),
            dma((2, 8)),
            dma((2, 8)),
            dma((2, 3)),
            dma((2, 3)),
            dma((2, 16)),
            dma((2, 16)),
        ],
        compiler_params=pltpu.CompilerParams(
            collective_id=0, has_side_effects=True, vmem_limit_bytes=60 * 2**20
        ),
        cost_estimate=pl.CostEstimate(flops=10**9, bytes_accessed=10**6, transcendentals=10**6),
    )(
        prod_radius.reshape(1, -1),
        prod_weight.reshape(1, -1),
        react_radius.reshape(1, -1),
        angle_cos.reshape(1, -1),
        angle_weight.reshape(1, -1),
        coupling.reshape(1, -1),
        react_basis,
        prod_basis,
    )
    return full.T


def solution(mesh):
    return jax.shard_map(
        local,
        mesh=mesh,
        in_specs=(P("blk", "chan", None), P("blk", "chan", None), P(), P(), P(), P(), P(), P("blk", "chan")),
        out_specs=P("blk", "chan"),
        check_vma=False,
    )
```

```python
import jax
import jax.numpy as jnp
from jax import lax
from jax.experimental import pallas as pl
from jax.experimental.pallas import tpu as pltpu
from jax.sharding import PartitionSpec as P

MESH = pl.DeviceIdType.MESH
F32 = jnp.float32
BF16 = jnp.bfloat16

turns_per_unit = 76.39437268410976
cos_terms = (
    0.9999999890590228,
    -19.739204499454026,
    64.93911745990036,
    -85.45013953095037,
    60.16763095136588,
    -25.96759924965491,
    6.528658162567069,
)
y_order = (2, 1, 3)
parts = 4
depth = 64 // parts


def lanes(a, b):
    return jnp.concatenate([a, b], axis=1)


def kernel(
    pr_any,
    pw_any,
    rr_any,
    cos_any,
    aw_any,
    cp_any,
    r_any,
    p_any,
    o_ref,
    pr_ref,
    pw_ref,
    rr_ref,
    cos_ref,
    aw_ref,
    cp_ref,
    r_ref,
    p_ref,
    s_r,
    s_p,
    pr_t,
    pw_t,
    rr_t,
    near_t,
    rz_send,
    rz_got,
    r_row,
    rhs,
    p_send,
    p_got,
    weight,
    in_send,
    in_got,
    in_row,
    y_send,
    y_got,
    own,
    z_send,
    z_got,
    in_sem,
    rz_ss,
    rz_rs,
    rb_ss,
    rb_rs,
    rc_ss,
    rc_rs,
    pb_ss,
    pb_rs,
    iz_ss,
    iz_rs,
    ir_ss,
    ir_rs,
    y_ss,
    y_rs,
    z_ss,
    z_rs,
):
    b = lax.axis_index("blk")
    h = lax.axis_index("chan")
    z, xh = h // 2, h % 2
    xl, y, co = b // 8, (b // 2) % 4, b % 2
    quad = xl * 2 + co
    me = xh * 4 + quad

    def at_blk(off):
        return ((b + off) % 16, h)

    def at_z(off):
        return (b, ((z + off) % 16) * 2 + xh)

    def at_y(t):
        return (xl * 8 + ((y + y_order[t]) % 4) * 2 + co, h)

    def remote(src, dst, ss, rs, dev):
        return pltpu.make_async_remote_copy(
            src_ref=src, dst_ref=dst, send_sem=ss, recv_sem=rs, device_id=dev, device_id_type=MESH
        )

    def row_peer(off):
        j = (me + off) % 8
        return j, (((j // 2) % 2) * 8 + y * 2 + j % 2, z * 2 + j // 4)

    loads = [
        pltpu.make_async_copy(src, dst, in_sem.at[n])
        for n, (src, dst) in enumerate(
            [
                (r_any, r_ref),
                (p_any, p_ref),
                (pr_any, pr_ref),
                (pw_any, pw_ref),
                (rr_any, rr_ref),
                (cos_any, cos_ref),
                (aw_any, aw_ref),
                (cp_any, cp_ref),
            ]
        )
    ]
    for load in loads:
        load.start()

    barrier = pltpu.get_barrier_semaphore()

    @pl.loop(1, 16)
    def _(off):
        pl.semaphore_signal(barrier, inc=1, device_id=at_z(off), device_id_type=MESH)
        pl.semaphore_signal(barrier, inc=1, device_id=at_blk(off), device_id_type=MESH)

    @pl.loop(0, 4)
    def _(i):
        dev = ((i // 2) * 8 + y * 2 + i % 2, z * 2 + 1 - xh)
        pl.semaphore_signal(barrier, inc=1, device_id=dev, device_id_type=MESH)

    loads[0].wait()

    @pl.loop(0, 8)
    def _(n):
        t = r_ref[pl.ds(2 * n, 2)].reshape(128, 128).astype(F32).T
        lo, hi = t[:64], t[64:]
        s_r[pl.ds(2 * n, 64, stride=16), :] = lanes(lo[:, :64], hi[:, :64])
        s_r[pl.ds(2 * n + 1, 64, stride=16), :] = lanes(lo[:, 64:], hi[:, 64:])

    for e in range(2):
        for j in range(8):
            at = j * 128 + e * 64
            rz_send[e, j] = s_r[at : at + 64, :].astype(BF16).reshape(4, 16, 128)

    pl.semaphore_wait(barrier, 34)

    for e in range(2):

        @pl.loop(0, 8)
        def _(off):
            j = (z // 2 + off) % 8
            k = j * 2 + co

            @pl.when(k != z)
            def _():
                remote(
                    rz_send.at[e, j], rz_got.at[e, z], rz_ss.at[e, j], rz_rs.at[e, z], (b, k * 2 + xh)
                ).start()

            @pl.when(k == z)
            def _():
                rz_got[e, z] = rz_send[e, j]

    loads[1].wait()

    @pl.loop(0, 16)
    def _(i):
        x = jnp.concatenate([p_ref[i], p_ref[16 + i]], axis=0)
        s_p[pl.ds(i, 128, stride=16), :] = x.astype(F32).T

    @pl.loop(0, 16)
    def _(off):
        d = (b + off) % 16
        for j in range(8):
            start = pl.multiple_of(((d % 2) * 64 + j * 8 + d // 2) * 16, 16)
            p_send[d, 16 * j : 16 * j + 16, :] = s_p[pl.ds(start, 16), :].astype(BF16)

        @pl.when(off > 0)
        def _():
            remote(p_send.at[d], p_got.at[b], pb_ss.at[off], pb_rs.at[b], at_blk(off)).start()

    p_got[b] = p_send[b]

    for load in loads[2:]:
        load.wait()
    for k in range(4):
        cols = slice(128 * k, 128 * k + 128)
        pr_t[cols, :] = jnp.broadcast_to(pr_ref[:, cols], (128, 128)).T
        pw_t[cols, :] = jnp.broadcast_to(pw_ref[:, cols], (128, 128)).T
    for k in range(2):
        cols = slice(128 * k, 128 * k + 128)
        rr_t[cols, :] = jnp.broadcast_to(rr_ref[:, cols], (128, 128)).T
    for k in range(16):
        at = (k % 2) * 128 + (k // 2) * 16
        near_t[at : at + 16, :] = rr_t[16 * k : 16 * k + 16, :]
    for k in range(2):
        cols = slice(128 * k, 128 * k + 128)
        rr_t[cols, :] = near_t[cols, :].T

    @pl.loop(0, 8)
    def _(gi):
        g = co * 64 + gi * 8 + b // 2
        two_cos = 2.0 * cos_ref[0, g]
        ang = aw_ref[0, g]

        @pl.loop(0, 16)
        def _(src):
            for sh in range(2):
                rows = pl.ds(pl.multiple_of(src * 32 + sh * 16, 16), 16)
                far = pr_t[rows, :]
                scale = pw_t[rows, :] * ang
                far2 = far * far
                for half in range(2):
                    near = rr_t[128 * half : 128 * half + 16, :]
                    q = (1.0 + near * near) + far2 - (two_cos * near) * far
                    rs = lax.rsqrt(q)
                    root = q * rs
                    root = root + (0.5 * rs) * (q - root * root)
                    turns = root * turns_per_unit
                    f = turns - jnp.round(turns)
                    u = f * f
                    c = jnp.full_like(u, cos_terms[6])
                    for term in cos_terms[5::-1]:
                        c = c * u + term
                    w = scale * c * (rs * rs)
                    w_hi = w.astype(BF16)
                    w_lo = (w - w_hi.astype(F32)).astype(BF16)
                    at = pl.multiple_of(sh * 256 + src * 16, 16)
                    cols = slice(128 * half, 128 * half + 128)
                    weight[gi, pl.ds(at, 16), cols] = w_hi
                    weight[gi, pl.ds(at + 512, 16), cols] = w_lo

    holder = co == z % 2

    def react_to_rows(e):
        @pl.when(holder)
        def _():
            @pl.loop(1, 16)
            def _(off):
                src = (z + off) % 16
                remote(
                    rz_send.at[e, 0], rz_got.at[e, src], rz_ss.at[e, 0], rz_rs.at[e, src], at_z(1)
                ).wait_recv()

            rows = pl.ds(pl.multiple_of((b // 2) * 16, 16), 16)

            @pl.loop(1, 8)
            def _(off):
                d = (b + 2 * off) % 16
                remote(
                    rz_got.at[e, :, (d // 2) % 4],
                    r_row.at[e, :, rows],
                    rb_ss.at[e, off],
                    rb_rs.at[e, b // 2],
                    at_blk(2 * off),
                ).start()

            r_row[e, :, rows] = rz_got[e, :, y]

    def other_core():
        return (b + 1 - 2 * co, h)

    def react_to_core(e):
        @pl.when(holder)
        def _():
            @pl.loop(1, 8)
            def _(off):
                n = (b // 2 + off) % 8
                rows = pl.ds(pl.multiple_of(n * 16, 16), 16)
                remote(
                    rz_got.at[e, :, 0], r_row.at[e, :, rows], rb_ss.at[e, 0], rb_rs.at[e, n], at_blk(2)
                ).wait_recv()

            remote(r_row.at[e], r_row.at[e], rc_ss.at[e], rc_rs.at[e], other_core()).start()

    react_to_rows(0)

    @pl.loop(1, 16)
    def _(off):
        src = (b + off) % 16
        remote(p_send.at[0], p_got.at[src], pb_ss.at[0], pb_rs.at[src], at_blk(1)).wait_recv()

    def in_place(k):
        return in_got.at[k // 8, (k // 2) % 4, k % 2]

    def send_integral(k, e):
        rows = slice(depth * e, depth * e + depth)

        @pl.when(k != z)
        def _():
            remote(
                in_send.at[k, rows], in_place(z).at[rows], iz_ss.at[e, k], iz_rs.at[e, z], (b, k * 2 + xh)
            ).start()

    @pl.loop(0, 8)
    def _(t):
        j = (z // 2 + 4 + t) % 8
        x = p_got[:, pl.ds(pl.multiple_of(16 * j, 16), 16), :].reshape(256, 128)
        xt = x.T
        lhs = jnp.concatenate([xt[:64], xt[64:], xt[:64], xt[64:]], axis=1)
        part = jnp.dot(lhs, weight[j], preferred_element_type=F32)
        for n in range(2):
            in_send[j * 2 + n] = part[:, 128 * n : 128 * n + 128].astype(BF16)
            send_integral(j * 2 + n, 0)

    for e in range(1, parts):

        @pl.loop(0, 16)
        def _(n):
            send_integral(((z // 2 + 4) * 2 + n) % 16, e)

    in_got[z // 8, (z // 2) % 4, z % 2] = in_send[z]

    react_to_rows(1)
    react_to_core(0)

    row_cols = pl.ds(pl.multiple_of(quad * 128, 128), 128)

    def integrals_to_row(e):
        rows = slice(depth * e, depth * e + depth)

        @pl.loop(1, 16)
        def _(off):
            src = (z + off) % 16
            remote(
                in_send.at[0, rows], in_place(src).at[rows], iz_ss.at[e, 0], iz_rs.at[e, src], at_z(1)
            ).wait_recv()

        at = pl.ds(pl.multiple_of(xh * depth, depth), depth)

        @pl.loop(1, 8)
        def _(off):
            j, dev = row_peer(off)
            remote(
                in_got.at[(j // 2) % 2, :, j % 2, rows],
                in_row.at[e, :, at, row_cols],
                ir_ss.at[e, off],
                ir_rs.at[e, me],
                dev,
            ).start()

        in_row[e, :, at, row_cols] = in_got[xl, :, co, rows]

    integrals_to_row(0)
    react_to_core(1)

    for e in range(2):

        @pl.when(jnp.logical_not(holder))
        def _():
            remote(r_row.at[e], r_row.at[e], rc_ss.at[e], rc_rs.at[e], other_core()).wait_recv()

        @pl.loop(0, 8)
        def _(n):
            x0 = r_row[e, 2 * n]
            x1 = r_row[e, 2 * n + 1]
            cols = pl.ds(pl.multiple_of(n * 128, 128), 128)
            rhs[256 * e : 256 * e + 128, cols] = lanes(x0[:, :64], x1[:, :64])
            rhs[256 * e + 128 : 256 * e + 256, cols] = lanes(x0[:, 64:], x1[:, 64:])

    def share(e):
        @pl.loop(1, 8)
        def _(off):
            j, dev = row_peer(off)
            at = pl.ds(pl.multiple_of((j // 4) * depth, depth), depth)
            cols = pl.ds(pl.multiple_of((j % 4) * 128, 128), 128)
            remote(
                in_got.at[0, :, 0, 0:depth], in_row.at[e, :, at, cols], ir_ss.at[e, 0], ir_rs.at[e, j], dev
            ).wait_recv()

        @pl.loop(0, 4)
        def _(n):
            cols = pl.ds(pl.multiple_of(n * 256, 256), 256)
            part = jnp.dot(in_row[e].reshape(8 * depth, 512), rhs[:, cols], preferred_element_type=F32)
            own[e, :, cols] = part
            y_send[e, :, :, cols] = part.astype(BF16).reshape(4, 2 * depth, 256)

        for t in range(3):
            yt = (y + y_order[t]) % 4
            remote(y_send.at[e, yt], y_got.at[e, t], y_ss.at[e, t], y_rs.at[e, t], at_y(t)).start()

    def plane_sum(e):
        for t in range(3):
            remote(y_send.at[e, 0], y_got.at[e, t], y_ss.at[e, t], y_rs.at[e, t], at_y(t)).wait_recv()

        @pl.loop(0, 8)
        def _(i):
            n = (z // 2 + 4 + i) % 8
            cols = pl.ds(pl.multiple_of(n * 128, 128), 128)
            s = own[e, pl.ds(pl.multiple_of(y * (2 * depth), 2 * depth), 2 * depth), cols]
            for t in range(3):
                s = s + y_got[e, t, :, cols].astype(F32)
            z_send[e, 2 * n] = lanes(s[:depth, :64], s[depth:, :64]).astype(BF16)
            z_send[e, 2 * n + 1] = lanes(s[:depth, 64:], s[depth:, 64:]).astype(BF16)

            @pl.loop(0, 2)
            def _(m):
                k = 2 * n + m

                @pl.when(k != z)
                def _():
                    remote(
                        z_send.at[e, k], z_got.at[e, z], z_ss.at[e, k], z_rs.at[e, z], (b, k * 2 + xh)
                    ).start()

                @pl.when(k == z)
                def _():
                    z_got[e, z] = z_send[e, z]

    for n in range(1, parts + 2):
        if n < parts:
            integrals_to_row(n)
        if n <= parts:
            share(n - 1)
        if n >= 2:
            plane_sum(n - 2)

    totals = []
    for e in range(parts):

        @pl.loop(1, 16)
        def _(off):
            src = (z + off) % 16
            remote(z_send.at[e, 0], z_got.at[e, src], z_ss.at[e, 0], z_rs.at[e, src], at_z(1)).wait_recv()

        total = z_got[e, 0].astype(F32)
        for k in range(1, 16):
            total = total + z_got[e, k].astype(F32)
        totals.append(total)
    out = jnp.concatenate(totals, axis=0).T
    o_ref[...] = lanes(out[:64] * cp_ref[0, 0].astype(F32), out[64:] * cp_ref[0, 1].astype(F32))

    @pl.loop(1, 16)
    def _(off):
        k = (z + off) % 16
        remote(p_send.at[0], p_got.at[0], pb_ss.at[off], pb_rs.at[0], at_blk(1)).wait_send()
        for e in range(parts):
            part = in_send.at[0, 0:depth]
            remote(part, part, iz_ss.at[e, k], iz_rs.at[e, 0], at_z(1)).wait_send()
            remote(z_send.at[e, 0], z_got.at[e, 0], z_ss.at[e, k], z_rs.at[e, 0], at_z(1)).wait_send()

    for e in range(2):

        @pl.loop(0, 8)
        def _(j):
            @pl.when(j * 2 + co != z)
            def _():
                remote(rz_send.at[e, j], rz_send.at[e, j], rz_ss.at[e, j], rz_rs.at[e, 0], at_z(1)).wait_send()

        @pl.when(holder)
        def _():
            @pl.loop(1, 8)
            def _(off):
                some = rz_got.at[e, :, 0]
                remote(some, some, rb_ss.at[e, off], rb_rs.at[e, 0], at_blk(1)).wait_send()

            remote(r_row.at[e], r_row.at[e], rc_ss.at[e], rc_rs.at[e], other_core()).wait_send()

    for e in range(parts):

        @pl.loop(1, 8)
        def _(off):
            part = in_got.at[0, :, 0, 0:depth]
            remote(part, part, ir_ss.at[e, off], ir_rs.at[e, 0], at_blk(1)).wait_send()

        for t in range(3):
            remote(y_send.at[e, 0], y_got.at[e, t], y_ss.at[e, t], y_rs.at[e, t], at_blk(1)).wait_send()


def local(react_basis, prod_basis, react_radius, prod_radius, prod_weight, angle_cos, angle_weight, coupling):
    dma = pltpu.SemaphoreType.DMA
    anywhere = pl.BlockSpec(memory_space=pl.ANY)
    full = pl.pallas_call(
        kernel,
        out_shape=jax.ShapeDtypeStruct((64, 128), F32),
        in_specs=[anywhere] * 8,
        out_specs=pl.BlockSpec(memory_space=pltpu.VMEM),
        scratch_shapes=[
            pltpu.VMEM((1, 512), F32),
            pltpu.VMEM((1, 512), F32),
            pltpu.VMEM((1, 256), F32),
            pltpu.SMEM((1, 128), F32),
            pltpu.SMEM((1, 128), F32),
            pltpu.SMEM((1, 2), jnp.int32),
            pltpu.VMEM((16, 64, 128), BF16),
            pltpu.VMEM((32, 64, 128), BF16),
            pltpu.VMEM((1024, 128), F32),
            pltpu.VMEM((2048, 128), F32),
            pltpu.VMEM((512, 128), F32),
            pltpu.VMEM((512, 128), F32),
            pltpu.VMEM((256, 128), F32),
            pltpu.VMEM((256, 128), F32),
            pltpu.VMEM((2, 8, 4, 16, 128), BF16),
            pltpu.VMEM((2, 16, 4, 16, 128), BF16),
            pltpu.VMEM((2, 16, 128, 128), BF16),
            pltpu.VMEM((512, 1024), BF16),
            pltpu.VMEM((16, 128, 128), BF16),
            pltpu.VMEM((16, 128, 128), BF16),
            pltpu.VMEM((8, 1024, 256), BF16),
            pltpu.VMEM((16, 64, 128), BF16),
            pltpu.VMEM((2, 4, 2, 64, 128), BF16),
            pltpu.VMEM((parts, 4, 2 * depth, 512), BF16),
            pltpu.VMEM((parts, 4, 2 * depth, 1024), BF16),
            pltpu.VMEM((parts, 3, 2 * depth, 1024), BF16),
            pltpu.VMEM((parts, 8 * depth, 1024), F32),
            pltpu.VMEM((parts, 16, depth, 128), BF16),
            pltpu.VMEM((parts, 16, depth, 128), BF16),
            dma((8,)),
            dma((2, 8)),
            dma((2, 16)),
            dma((2, 8)),
            dma((2, 8)),
            dma((2,)),
            dma((2,)),
            dma((16,)),
            dma((16,)),
            dma((parts, 16)),
            dma((parts, 16)),
            dma((parts, 8)),
            dma((parts, 8)),
            dma((parts, 3)),
            dma((parts, 3)),
            dma((parts, 16)),
            dma((parts, 16)),
        ],
        compiler_params=pltpu.CompilerParams(
            collective_id=0, has_side_effects=True, vmem_limit_bytes=60 * 2**20
        ),
        cost_estimate=pl.CostEstimate(flops=10**9, bytes_accessed=10**6, transcendentals=10**6),
    )(
        prod_radius.reshape(1, -1),
        prod_weight.reshape(1, -1),
        react_radius.reshape(1, -1),
        angle_cos.reshape(1, -1),
        angle_weight.reshape(1, -1),
        coupling.reshape(1, -1),
        react_basis,
        prod_basis,
    )
    return full.T


def solution(mesh):
    return jax.shard_map(
        local,
        mesh=mesh,
        in_specs=(P("blk", "chan", None), P("blk", "chan", None), P(), P(), P(), P(), P(), P("blk", "chan")),
        out_specs=P("blk", "chan"),
        check_vma=False,
    )
```

```python
import jax
import jax.numpy as jnp
from jax import lax
from jax.experimental import pallas as pl
from jax.experimental.pallas import tpu as pltpu
from jax.sharding import PartitionSpec as P

MESH = pl.DeviceIdType.MESH
F32 = jnp.float32
BF16 = jnp.bfloat16

turns_per_unit = 76.39437268410976
cos_terms = (
    0.9999999890590228,
    -19.739204499454026,
    64.93911745990036,
    -85.45013953095037,
    60.16763095136588,
    -25.96759924965491,
    6.528658162567069,
)
y_order = (2, 1, 3)
parts = 4
depth = 64 // parts


def far_first(half, t):
    return half + (1 - 2 * (t % 2)) * ((t + 1) // 2)


def lanes(a, b):
    return jnp.concatenate([a, b], axis=1)


def kernel(
    pr_any,
    pw_any,
    rr_any,
    cos_any,
    aw_any,
    cp_any,
    r_any,
    p_any,
    o_ref,
    pr_ref,
    pw_ref,
    rr_ref,
    cos_ref,
    aw_ref,
    cp_ref,
    r_ref,
    p_ref,
    s_r,
    s_p,
    pr_t,
    pw_t,
    rr_t,
    near_t,
    rz_send,
    rz_got,
    r_row,
    rhs,
    p_send,
    p_got,
    weight,
    in_send,
    in_got,
    in_row,
    y_send,
    y_got,
    own,
    z_send,
    z_got,
    in_sem,
    rz_ss,
    rz_rs,
    rb_ss,
    rb_rs,
    rc_ss,
    rc_rs,
    pb_ss,
    pb_rs,
    iz_ss,
    iz_rs,
    ir_ss,
    ir_rs,
    y_ss,
    y_rs,
    z_ss,
    z_rs,
):
    b = lax.axis_index("blk")
    h = lax.axis_index("chan")
    z, xh = h // 2, h % 2
    xl, y, co = b // 8, (b // 2) % 4, b % 2
    quad = xl * 2 + co
    me = xh * 4 + quad

    def at_blk(off):
        return ((b + off) % 16, h)

    def at_z(off):
        return (b, ((z + off) % 16) * 2 + xh)

    def at_y(t):
        return (xl * 8 + ((y + y_order[t]) % 4) * 2 + co, h)

    def remote(src, dst, ss, rs, dev):
        return pltpu.make_async_remote_copy(
            src_ref=src, dst_ref=dst, send_sem=ss, recv_sem=rs, device_id=dev, device_id_type=MESH
        )

    def row_peer(off):
        j = (me + off) % 8
        return j, (((j // 2) % 2) * 8 + y * 2 + j % 2, z * 2 + j // 4)

    loads = [
        pltpu.make_async_copy(src, dst, in_sem.at[n])
        for n, (src, dst) in enumerate(
            [
                (r_any, r_ref),
                (p_any, p_ref),
                (pr_any, pr_ref),
                (pw_any, pw_ref),
                (rr_any, rr_ref),
                (cos_any, cos_ref),
                (aw_any, aw_ref),
                (cp_any, cp_ref),
            ]
        )
    ]
    for load in loads:
        load.start()

    barrier = pltpu.get_barrier_semaphore()

    @pl.loop(1, 16)
    def _(off):
        pl.semaphore_signal(barrier, inc=1, device_id=at_z(off), device_id_type=MESH)
        pl.semaphore_signal(barrier, inc=1, device_id=at_blk(off), device_id_type=MESH)

    @pl.loop(0, 4)
    def _(i):
        dev = ((i // 2) * 8 + y * 2 + i % 2, z * 2 + 1 - xh)
        pl.semaphore_signal(barrier, inc=1, device_id=dev, device_id_type=MESH)

    loads[0].wait()

    @pl.loop(0, 8)
    def _(n):
        t = r_ref[pl.ds(2 * n, 2)].reshape(128, 128).astype(F32).T
        lo, hi = t[:64], t[64:]
        s_r[pl.ds(2 * n, 64, stride=16), :] = lanes(lo[:, :64], hi[:, :64])
        s_r[pl.ds(2 * n + 1, 64, stride=16), :] = lanes(lo[:, 64:], hi[:, 64:])

    for e in range(2):
        for j in range(8):
            at = j * 128 + e * 64
            rz_send[e, j] = s_r[at : at + 64, :].astype(BF16).reshape(4, 16, 128)

    pl.semaphore_wait(barrier, 34)

    for e in range(2):

        @pl.loop(0, 8)
        def _(off):
            j = (z // 2 + far_first(4, off)) % 8
            k = j * 2 + co

            @pl.when(k != z)
            def _():
                remote(
                    rz_send.at[e, j], rz_got.at[e, z], rz_ss.at[e, j], rz_rs.at[e, z], (b, k * 2 + xh)
                ).start()

            @pl.when(k == z)
            def _():
                rz_got[e, z] = rz_send[e, j]

    loads[1].wait()

    @pl.loop(0, 16)
    def _(i):
        x = jnp.concatenate([p_ref[i], p_ref[16 + i]], axis=0)
        s_p[pl.ds(i, 128, stride=16), :] = x.astype(F32).T

    @pl.loop(0, 16)
    def _(off):
        d = (b + off) % 16
        for j in range(8):
            start = pl.multiple_of(((d % 2) * 64 + j * 8 + d // 2) * 16, 16)
            p_send[d, 16 * j : 16 * j + 16, :] = s_p[pl.ds(start, 16), :].astype(BF16)

        @pl.when(off > 0)
        def _():
            remote(p_send.at[d], p_got.at[b], pb_ss.at[off], pb_rs.at[b], at_blk(off)).start()

    p_got[b] = p_send[b]

    for load in loads[2:]:
        load.wait()
    for k in range(4):
        cols = slice(128 * k, 128 * k + 128)
        pr_t[cols, :] = jnp.broadcast_to(pr_ref[:, cols], (128, 128)).T
        pw_t[cols, :] = jnp.broadcast_to(pw_ref[:, cols], (128, 128)).T
    for k in range(2):
        cols = slice(128 * k, 128 * k + 128)
        rr_t[cols, :] = jnp.broadcast_to(rr_ref[:, cols], (128, 128)).T
    for k in range(16):
        at = (k % 2) * 128 + (k // 2) * 16
        near_t[at : at + 16, :] = rr_t[16 * k : 16 * k + 16, :]
    for k in range(2):
        cols = slice(128 * k, 128 * k + 128)
        rr_t[cols, :] = near_t[cols, :].T

    @pl.loop(0, 8)
    def _(gi):
        g = co * 64 + gi * 8 + b // 2
        two_cos = 2.0 * cos_ref[0, g]
        ang = aw_ref[0, g]

        @pl.loop(0, 16)
        def _(src):
            for sh in range(2):
                rows = pl.ds(pl.multiple_of(src * 32 + sh * 16, 16), 16)
                far = pr_t[rows, :]
                scale = pw_t[rows, :] * ang
                far2 = far * far
                for half in range(2):
                    near = rr_t[128 * half : 128 * half + 16, :]
                    q = (1.0 + near * near) + far2 - (two_cos * near) * far
                    rs = lax.rsqrt(q)
                    root = q * rs
                    root = root + (0.5 * rs) * (q - root * root)
                    turns = root * turns_per_unit
                    f = turns - jnp.round(turns)
                    u = f * f
                    c = jnp.full_like(u, cos_terms[6])
                    for term in cos_terms[5::-1]:
                        c = c * u + term
                    w = scale * c * (rs * rs)
                    w_hi = w.astype(BF16)
                    w_lo = (w - w_hi.astype(F32)).astype(BF16)
                    at = pl.multiple_of(sh * 256 + src * 16, 16)
                    cols = slice(128 * half, 128 * half + 128)
                    weight[gi, pl.ds(at, 16), cols] = w_hi
                    weight[gi, pl.ds(at + 512, 16), cols] = w_lo

    holder = co == z % 2

    def react_to_rows(e):
        @pl.when(holder)
        def _():
            @pl.loop(1, 16)
            def _(off):
                src = (z + off) % 16
                remote(
                    rz_send.at[e, 0], rz_got.at[e, src], rz_ss.at[e, 0], rz_rs.at[e, src], at_z(1)
                ).wait_recv()

            rows = pl.ds(pl.multiple_of((b // 2) * 16, 16), 16)

            @pl.loop(1, 8)
            def _(off):
                d = (b + 2 * off) % 16
                remote(
                    rz_got.at[e, :, (d // 2) % 4],
                    r_row.at[e, :, rows],
                    rb_ss.at[e, off],
                    rb_rs.at[e, b // 2],
                    at_blk(2 * off),
                ).start()

            r_row[e, :, rows] = rz_got[e, :, y]

    def other_core():
        return (b + 1 - 2 * co, h)

    def react_to_core(e):
        @pl.when(holder)
        def _():
            @pl.loop(1, 8)
            def _(off):
                n = (b // 2 + off) % 8
                rows = pl.ds(pl.multiple_of(n * 16, 16), 16)
                remote(
                    rz_got.at[e, :, 0], r_row.at[e, :, rows], rb_ss.at[e, 0], rb_rs.at[e, n], at_blk(2)
                ).wait_recv()

            remote(r_row.at[e], r_row.at[e], rc_ss.at[e], rc_rs.at[e], other_core()).start()

    react_to_rows(0)

    @pl.loop(1, 16)
    def _(off):
        src = (b + off) % 16
        remote(p_send.at[0], p_got.at[src], pb_ss.at[0], pb_rs.at[src], at_blk(1)).wait_recv()

    def in_place(k):
        return in_got.at[k // 8, (k // 2) % 4, k % 2]

    def send_integral(k, e):
        rows = slice(depth * e, depth * e + depth)

        @pl.when(k != z)
        def _():
            remote(
                in_send.at[k, rows], in_place(z).at[rows], iz_ss.at[e, k], iz_rs.at[e, z], (b, k * 2 + xh)
            ).start()

    @pl.loop(0, 8, unroll=2)
    def _(t):
        j = (z // 2 + far_first(4, t)) % 8
        x = p_got[:, pl.ds(pl.multiple_of(16 * j, 16), 16), :].reshape(256, 128)
        xt = x.T
        lhs = jnp.concatenate([xt[:64], xt[64:], xt[:64], xt[64:]], axis=1)
        part = jnp.dot(lhs, weight[j], preferred_element_type=F32)
        for n in range(2):
            in_send[j * 2 + n] = part[:, 128 * n : 128 * n + 128].astype(BF16)
            send_integral(j * 2 + n, 0)

    for e in range(1, parts):

        @pl.loop(0, 15)
        def _(t):
            off = far_first(8, t)
            k = (z + off) % 16
            rows = slice(depth * e, depth * e + depth)
            remote(
                in_send.at[k, rows], in_place(z).at[rows], iz_ss.at[e, k], iz_rs.at[e, z], at_z(off)
            ).start()

    in_got[z // 8, (z // 2) % 4, z % 2] = in_send[z]

    react_to_rows(1)
    react_to_core(0)

    row_cols = pl.ds(pl.multiple_of(quad * 128, 128), 128)

    def integrals_to_row(e):
        rows = slice(depth * e, depth * e + depth)

        @pl.loop(1, 16)
        def _(off):
            src = (z + off) % 16
            remote(
                in_send.at[0, rows], in_place(src).at[rows], iz_ss.at[e, 0], iz_rs.at[e, src], at_z(1)
            ).wait_recv()

        at = pl.ds(pl.multiple_of(xh * depth, depth), depth)

        @pl.loop(1, 8)
        def _(off):
            j, dev = row_peer(off)
            remote(
                in_got.at[(j // 2) % 2, :, j % 2, rows],
                in_row.at[e, :, at, row_cols],
                ir_ss.at[e, off],
                ir_rs.at[e, me],
                dev,
            ).start()

        in_row[e, :, at, row_cols] = in_got[xl, :, co, rows]

    integrals_to_row(0)
    react_to_core(1)

    for e in range(2):

        @pl.when(jnp.logical_not(holder))
        def _():
            remote(r_row.at[e], r_row.at[e], rc_ss.at[e], rc_rs.at[e], other_core()).wait_recv()

        @pl.loop(0, 8)
        def _(n):
            x0 = r_row[e, 2 * n]
            x1 = r_row[e, 2 * n + 1]
            cols = pl.ds(pl.multiple_of(n * 128, 128), 128)
            rhs[256 * e : 256 * e + 128, cols] = lanes(x0[:, :64], x1[:, :64])
            rhs[256 * e + 128 : 256 * e + 256, cols] = lanes(x0[:, 64:], x1[:, 64:])

    def share(e):
        @pl.loop(1, 8)
        def _(off):
            j, dev = row_peer(off)
            at = pl.ds(pl.multiple_of((j // 4) * depth, depth), depth)
            cols = pl.ds(pl.multiple_of((j % 4) * 128, 128), 128)
            remote(
                in_got.at[0, :, 0, 0:depth], in_row.at[e, :, at, cols], ir_ss.at[e, 0], ir_rs.at[e, j], dev
            ).wait_recv()

        for n in range(4):
            cols = slice(256 * n, 256 * n + 256)
            part = jnp.dot(in_row[e].reshape(8 * depth, 512), rhs[:, cols], preferred_element_type=F32)
            own[e, :, cols] = part
            y_send[e, :, :, cols] = part.astype(BF16).reshape(4, 2 * depth, 256)

        for t in range(3):
            yt = (y + y_order[t]) % 4
            remote(y_send.at[e, yt], y_got.at[e, t], y_ss.at[e, t], y_rs.at[e, t], at_y(t)).start()

    def plane_sum(e):
        for t in range(3):
            remote(y_send.at[e, 0], y_got.at[e, t], y_ss.at[e, t], y_rs.at[e, t], at_y(t)).wait_recv()

        mine = pl.ds(pl.multiple_of(y * (2 * depth), 2 * depth), 2 * depth)
        for n in range(8):
            cols = slice(128 * n, 128 * n + 128)
            s = own[e, mine, cols]
            for t in range(3):
                s = s + y_got[e, t, :, cols].astype(F32)
            z_send[e, 2 * n] = lanes(s[:depth, :64], s[depth:, :64]).astype(BF16)
            z_send[e, 2 * n + 1] = lanes(s[:depth, 64:], s[depth:, 64:]).astype(BF16)

        @pl.loop(0, 15)
        def _(t):
            off = far_first(8, t)
            k = (z + off) % 16
            remote(z_send.at[e, k], z_got.at[e, z], z_ss.at[e, off], z_rs.at[e, z], at_z(off)).start()

        z_got[e, z] = z_send[e, z]

    for n in range(1, parts + 2):
        if n < parts:
            integrals_to_row(n)
        if n <= parts:
            share(n - 1)
        if n >= 2:
            plane_sum(n - 2)

    @pl.loop(1, 16)
    def _(off):
        k = (z + off) % 16
        remote(p_send.at[0], p_got.at[0], pb_ss.at[off], pb_rs.at[0], at_blk(1)).wait_send()
        for e in range(parts):
            part = in_send.at[0, 0:depth]
            remote(part, part, iz_ss.at[e, k], iz_rs.at[e, 0], at_z(1)).wait_send()

    for e in range(2):

        @pl.loop(0, 8)
        def _(j):
            @pl.when(j * 2 + co != z)
            def _():
                remote(rz_send.at[e, j], rz_send.at[e, j], rz_ss.at[e, j], rz_rs.at[e, 0], at_z(1)).wait_send()

        @pl.when(holder)
        def _():
            @pl.loop(1, 8)
            def _(off):
                some = rz_got.at[e, :, 0]
                remote(some, some, rb_ss.at[e, off], rb_rs.at[e, 0], at_blk(1)).wait_send()

            remote(r_row.at[e], r_row.at[e], rc_ss.at[e], rc_rs.at[e], other_core()).wait_send()

    for e in range(parts):

        @pl.loop(1, 8)
        def _(off):
            part = in_got.at[0, :, 0, 0:depth]
            remote(part, part, ir_ss.at[e, off], ir_rs.at[e, 0], at_blk(1)).wait_send()

        for t in range(3):
            remote(y_send.at[e, 0], y_got.at[e, t], y_ss.at[e, t], y_rs.at[e, t], at_blk(1)).wait_send()

    totals = []
    for e in range(parts):

        @pl.loop(1, 16)
        def _(off):
            src = (z + off) % 16
            remote(z_send.at[e, 0], z_got.at[e, src], z_ss.at[e, off], z_rs.at[e, src], at_z(1)).wait()

        total = z_got[e, 0].astype(F32)
        for k in range(1, 16):
            total = total + z_got[e, k].astype(F32)
        totals.append(total)
    out = jnp.concatenate(totals, axis=0).T
    o_ref[...] = lanes(out[:64] * cp_ref[0, 0].astype(F32), out[64:] * cp_ref[0, 1].astype(F32))


def local(react_basis, prod_basis, react_radius, prod_radius, prod_weight, angle_cos, angle_weight, coupling):
    dma = pltpu.SemaphoreType.DMA
    anywhere = pl.BlockSpec(memory_space=pl.ANY)
    full = pl.pallas_call(
        kernel,
        out_shape=jax.ShapeDtypeStruct((64, 128), F32),
        in_specs=[anywhere] * 8,
        out_specs=pl.BlockSpec(memory_space=pltpu.VMEM),
        scratch_shapes=[
            pltpu.VMEM((1, 512), F32),
            pltpu.VMEM((1, 512), F32),
            pltpu.VMEM((1, 256), F32),
            pltpu.SMEM((1, 128), F32),
            pltpu.SMEM((1, 128), F32),
            pltpu.SMEM((1, 2), jnp.int32),
            pltpu.VMEM((16, 64, 128), BF16),
            pltpu.VMEM((32, 64, 128), BF16),
            pltpu.VMEM((1024, 128), F32),
            pltpu.VMEM((2048, 128), F32),
            pltpu.VMEM((512, 128), F32),
            pltpu.VMEM((512, 128), F32),
            pltpu.VMEM((256, 128), F32),
            pltpu.VMEM((256, 128), F32),
            pltpu.VMEM((2, 8, 4, 16, 128), BF16),
            pltpu.VMEM((2, 16, 4, 16, 128), BF16),
            pltpu.VMEM((2, 16, 128, 128), BF16),
            pltpu.VMEM((512, 1024), BF16),
            pltpu.VMEM((16, 128, 128), BF16),
            pltpu.VMEM((16, 128, 128), BF16),
            pltpu.VMEM((8, 1024, 256), BF16),
            pltpu.VMEM((16, 64, 128), BF16),
            pltpu.VMEM((2, 4, 2, 64, 128), BF16),
            pltpu.VMEM((parts, 4, 2 * depth, 512), BF16),
            pltpu.VMEM((parts, 4, 2 * depth, 1024), BF16),
            pltpu.VMEM((parts, 3, 2 * depth, 1024), BF16),
            pltpu.VMEM((parts, 8 * depth, 1024), F32),
            pltpu.VMEM((parts, 16, depth, 128), BF16),
            pltpu.VMEM((parts, 16, depth, 128), BF16),
            dma((8,)),
            dma((2, 8)),
            dma((2, 16)),
            dma((2, 8)),
            dma((2, 8)),
            dma((2,)),
            dma((2,)),
            dma((16,)),
            dma((16,)),
            dma((parts, 16)),
            dma((parts, 16)),
            dma((parts, 8)),
            dma((parts, 8)),
            dma((parts, 3)),
            dma((parts, 3)),
            dma((parts, 16)),
            dma((parts, 16)),
        ],
        compiler_params=pltpu.CompilerParams(
            collective_id=0, has_side_effects=True, vmem_limit_bytes=60 * 2**20
        ),
        cost_estimate=pl.CostEstimate(flops=10**9, bytes_accessed=10**6, transcendentals=10**6),
    )(
        prod_radius.reshape(1, -1),
        prod_weight.reshape(1, -1),
        react_radius.reshape(1, -1),
        angle_cos.reshape(1, -1),
        angle_weight.reshape(1, -1),
        coupling.reshape(1, -1),
        react_basis,
        prod_basis,
    )
    return full.T


def solution(mesh):
    return jax.shard_map(
        local,
        mesh=mesh,
        in_specs=(P("blk", "chan", None), P("blk", "chan", None), P(), P(), P(), P(), P(), P("blk", "chan")),
        out_specs=P("blk", "chan"),
        check_vma=False,
    )
```
